128 devices in a mesh: row: 16 (over y_lo, x, core), col: 8 (over y_hi, z).
Axes of the slice: x: 4, y: 4 (y_hi: 2, y_lo: 2; y = y_hi * 2 + y_lo), z: 4, core: 2. Of those that a mesh axis runs over, the one named last changes fastest.
Arguments:
- eigvecs: float32 [8, 256, 131072], P('col', 'row'), may hold values from -6 to 6
- reflectors: float32 [8, 131072, 256], P('col', 'row'), may hold values from -6 to 6
- factors: float32 [8, 256, 256], P('col'), may hold values from -7.6293945e-06 to 3.0517578e-05, as said below
- owner: int32 [8], replicated, may hold values from 0 to 7, each once
Outputs:
- back_vectors: float32 [8, 256, 131072], P('col', None, 'row')
The draws below stay inside these ranges and needn't reach their ends.
Inputs may be any that keep to these rules, and one draw needn't show every extreme that they name: Each factors[c] is upper triangular with a positive diagonal.
All inputs are finite; a program needn't handle non-finite values.
Results may differ from the reference program's by a relative error of at most 0.0001.
Values sent between devices are 32-bit elements; how exact they have to be, the bound alone decides.
No kernel may reach another device: no remote copies, remote signals or barrier semaphores. Data moves between devices by JAX's collectives and lax.ppermute only.
A program may use at most 192 MiB of HBM per device.

```python
import jax
import jax.numpy as jnp
from jax import lax

N = 131072
NB = 256
MC = 256
N_COL = 8


def draw_factors(key, part):
    first, second = jax.random.split(key, 2)
    shape = (N_COL, NB, NB)
    diag_part = jax.random.uniform(first, (N_COL, NB), jnp.float32, 0.5, 1.5)
    upper_part = jnp.clip(0.1 * jax.random.normal(second, shape, jnp.float32), -0.5, 0.5)
    rows = lax.broadcasted_iota(jnp.int32, shape, 1)
    cols = lax.broadcasted_iota(jnp.int32, shape, 2)
    strict = (cols > rows).astype(jnp.float32)
    same = (cols == rows).astype(jnp.float32)
    matrix = upper_part * strict + diag_part[:, :, None] * same
    return 2.0 / N * matrix


def levels(rng, extent, cuts, smallest, high):
    level = 1.0
    for position, blocks in cuts:
        heights = jax.random.uniform(jax.random.fold_in(jax.random.fold_in(rng, 6), position), (blocks,), jnp.float32, smallest / len(cuts), high / len(cuts))
        level = level * jnp.repeat(jnp.exp(heights), extent[position] // blocks).reshape((-1,) + (1,) * (len(extent) - 1 - position))
    return level


def noise(stream_key, shape, scale, limit, shards=(), kind=jnp.bfloat16):
    entries = jax.random.normal(stream_key, shape, jnp.float32) * scale
    if len(shards) > 0:
        entries = levels(stream_key, shape, shards, -0.22, 0.18) * entries
    return jnp.clip(entries, min=-limit, max=limit).astype(kind)


def setup_inputs(seed: int = 0) -> dict:
    seeds = jax.random.split(jax.random.key(seed), 5)
    eigvecs = noise(seeds[0], (N_COL, MC, N), 1.0, 6.0, ((0, 8), (1, 16)), jnp.float32)
    reflectors = noise(seeds[1], (N_COL, N, NB), 1.0, 6.0, ((0, 8), (1, 16)), jnp.float32)
    factors = draw_factors(jax.random.fold_in(seeds[4], 71), 0)
    owner = jax.random.permutation(seeds[3], N_COL).astype(jnp.int32)
    return dict(eigvecs=eigvecs, reflectors=reflectors, factors=factors, owner=owner)


def build_panel(reflectors, factors, owner, block):
    chosen = owner[block]
    vectors = lax.dynamic_index_in_dim(reflectors, chosen, 0, keepdims=False)
    factor = lax.dynamic_index_in_dim(factors, chosen, 0, keepdims=False)
    rows = lax.broadcasted_iota(jnp.int32, (N, NB), 0)
    cols = lax.broadcasted_iota(jnp.int32, (N, NB), 1) + block * NB
    masked = jnp.where(rows > cols, vectors, jnp.zeros_like(vectors))
    masked = masked + (rows == cols).astype(vectors.dtype)
    return masked, factor


def reference(eigvecs, reflectors, factors, owner):
    exact = lax.Precision.HIGHEST
    field = eigvecs
    for block in (1, 0):
        vectors, factor = build_panel(reflectors, factors, owner, block)
        project = jnp.einsum("cmn,nk->cmk", field, vectors, precision=exact)
        update = jnp.einsum("cmk,jk->cmj", project, factor, precision=exact)
        field = field - jnp.einsum("cmj,nj->cmn", update, vectors, precision=exact)
    return field
```

```python
import functools

import jax
import jax.numpy as jnp
from jax import lax
from jax.experimental import pallas as pl
from jax.experimental.pallas import tpu as pltpu
from jax.sharding import PartitionSpec as P

RING = 4
GROUPS = 2
QUARTER = 2
CHUNKS = RING * QUARTER
SLOTS = max(CHUNKS + 2, 3 * QUARTER + 5)
STEPS = (1, -1)
VMEM = 48 * 2**20
FIELDS = 6
F32 = jnp.float32


def ring_pairs(step):
    return [(h * RING + z, h * RING + (z + step) % RING) for h in range(2) for z in range(RING)]


SWAP = [(i, (i + RING) % (2 * RING)) for i in range(2 * RING)]


def crossing_id(batch, place):
    return jnp.where(place == 0, 3 * QUARTER + batch, 3 * batch + 3 - place)


def cross_slots(s):
    send = next((b for b in range(QUARTER) if s == 3 * b + 3), None)
    inject = next((b for b in range(QUARTER) if s == 3 * b + 5), None)
    return send, inject


def plan(owner, step):
    me = lax.axis_index("col")
    far = me // RING != owner // RING
    place = jnp.remainder(step * (me - owner), RING)
    source = me == owner
    rows = []
    for s in range(SLOTS + 1):
        _, inject = cross_slots(s)
        near_id = s - place
        near_ok = (near_id >= 0) & (near_id < CHUNKS) & ~source
        if s == 0:
            near_ok = False
        far_id, far_ok = 0, False
        for b in range(QUARTER):
            j = s - 1 - (3 * b + 5)
            if 0 <= j < 3:
                far_id, far_ok = crossing_id(b, jnp.remainder(place - 1 - j, RING)), True
        good = jnp.where(far, far_ok, near_ok)
        index = jnp.where(good, jnp.where(far, far_id, near_id), -1)
        put = far if inject is not None else False
        cross = crossing_id(inject, place) if inject is not None else 0
        rows.append([source, ~source & ~jnp.asarray(put), index, put, cross, 0])
    return jnp.stack([jnp.stack([jnp.asarray(v).astype(jnp.int32) for v in r]) for r in rows])


def slot_body(s, group, n_cross_in, plan_ref, own_ref, *refs):
    refs = list(refs)
    heads = [refs.pop(0), refs.pop(0)] if group == 0 else [None, None]
    got = [refs.pop(0), refs.pop(0)] if s else [None, None]
    crossed = [refs.pop(0), refs.pop(0)] if n_cross_in else [None, None]
    refs.pop(0)
    refs.pop(0)
    held = [refs.pop(0), refs.pop(0)]
    send = [refs.pop(0), refs.pop(0)] if s < SLOTS else [None, None]
    over, _ = cross_slots(s)
    across = [refs.pop(0), refs.pop(0)] if over is not None else [None, None]
    sems = refs.pop(0)
    size = own_ref.shape[1] // (GROUPS * CHUNKS)

    copies = []
    for i in range(2):
        at = functools.partial(lambda i, f: plan_ref[i, s, f], i)
        source, relay, index, put, cross = (at(f) for f in range(5))

        def own(c):
            if c == 0 and group == 0:
                return heads[i]
            return own_ref.at[0, pl.ds((group * CHUNKS + c) * size, size)]

        def slot(index):
            return held[i].at[group * CHUNKS + index]

        if s < CHUNKS:
            copies.append((source == 1, own(s), slot(s)))
            copies.append((True if s == 0 else source == 1, own(s), send[i]))
        if s:
            copies.append((index >= 0, got[i], slot(jnp.maximum(index, 0))))
            if s < SLOTS:
                copies.append((relay == 1, got[i], send[i]))
        if n_cross_in:
            copies.append((put == 1, crossed[i], slot(cross)))
            copies.append((put == 1, crossed[i], send[i]))
        if over is not None:
            copies.append((source == 1, own(3 * QUARTER + over), across[i]))
            copies.append((source == 0, got[i], across[i]))

    def go(wait):
        for n, (when, src, dst) in enumerate(copies):
            copy = pltpu.make_async_copy(src, dst, sems.at[n])

            def act(copy=copy):
                copy.wait() if wait else copy.start()

            if when is True:
                act()
            else:
                pl.when(when)(act)

    go(False)
    go(True)


def slot_call(s, group, plans, own, heads, got, crossed, held):
    chunk = jax.ShapeDtypeStruct((own.shape[1] // (GROUPS * CHUNKS), own.shape[2]), own.dtype)
    over, inject = cross_slots(s)
    ins = [plans, own]
    if group == 0:
        ins += heads
    if s:
        ins += got
    if inject is not None:
        ins += crossed
    first = len(ins)
    ins += held
    outs = [jax.ShapeDtypeStruct(h.shape, h.dtype) for h in held]
    if s < SLOTS:
        outs += [chunk] * 2
    if over is not None:
        outs += [chunk] * 2
    any_spec = pl.BlockSpec(memory_space=pl.ANY)
    out = pl.pallas_call(
        functools.partial(slot_body, s, group, 1 if inject is not None else 0),
        out_shape=outs,
        in_specs=[pl.BlockSpec(memory_space=pltpu.SMEM)] + [any_spec] * (len(ins) - 1),
        out_specs=[any_spec] * len(outs),
        scratch_shapes=[pltpu.SemaphoreType.DMA((16,))],
        input_output_aliases={first: 0, first + 1: 1},
        cost_estimate=pl.CostEstimate(flops=0, bytes_accessed=4 * 2**20, transcendentals=0),
        name=f"slot{s}_{group}",
    )(*ins)
    held, out = out[:2], out[2:]
    send = across = None
    if s < SLOTS:
        send, out = out[:2], out[2:]
    if over is not None:
        across = out
    return held, send, across


def parts_of(x):
    high = x.astype(jnp.bfloat16)
    low = (x - high.astype(F32)).astype(jnp.bfloat16)
    return high, low


def dot3(left, right, dims):
    (lh, ll), (rh, rl) = left, right
    go = functools.partial(lax.dot_general, dimension_numbers=(dims, ((), ())), preferred_element_type=F32)
    return go(lh, rh) + (go(lh, rl) + go(ll, rh))


def full(left, right, dims):
    return lax.dot_general(
        left, right, (dims, ((), ())), precision=lax.Precision.HIGHEST, preferred_element_type=F32
    )


def project_body(xa_ref, xb_ref, p1_ref, p0_ref, out_ref):
    count, width = xa_ref.shape[0] * xa_ref.shape[1], p1_ref.shape[-1]
    x = jnp.concatenate([r[...].reshape(count, r.shape[-1]) for r in (xa_ref, xb_ref)], 0)
    x, p1, p0 = parts_of(x), parts_of(p1_ref[0]), parts_of(p0_ref[0])

    @pl.when(pl.program_id(0) == 0)
    def _():
        out_ref[...] = jnp.zeros_like(out_ref)

    out_ref[0] += dot3(x, p1, ((1,), (0,)))
    out_ref[1] += dot3(x, p0, ((1,), (0,)))
    out_ref[2] += dot3(p1, p0, ((0,), (0,)))


def project(xs, held):
    chunks, size, width = held[0].shape
    xspec = pl.BlockSpec((*xs[0].shape[:2], size), lambda i: (0, 0, i))
    pspec = pl.BlockSpec((1, size, width), lambda i: (i, 0, 0))
    return pl.pallas_call(
        project_body,
        out_shape=jax.ShapeDtypeStruct((3, width, width), F32),
        grid=(chunks,),
        in_specs=[xspec, xspec, pspec, pspec],
        out_specs=pl.BlockSpec((3, width, width), lambda i: (0, 0, 0)),
        compiler_params=pltpu.CompilerParams(vmem_limit_bytes=VMEM),
        name="project",
    )(*xs, *held)


def update_body(sum_ref, factor_ref, xa_ref, xb_ref, p1_ref, p0_ref, out_ref, y_ref):
    @pl.when(pl.program_id(0) == 0)
    def _():
        y1 = full(sum_ref[0], factor_ref[0], ((1,), (1,)))
        w0 = sum_ref[1] - full(y1, sum_ref[2], ((1,), (0,)))
        y0 = full(w0, factor_ref[1], ((1,), (1,)))
        for i, y in enumerate((y1, y0)):
            high, low = parts_of(y)
            y_ref[i, 0] = high
            y_ref[i, 1] = low

    change = 0
    for i, ref in enumerate((p1_ref, p0_ref)):
        change += dot3((y_ref[i, 0], y_ref[i, 1]), parts_of(ref[0]), ((1,), (1,)))
    half = change.shape[0] // 2
    for t, ref in enumerate((xa_ref, xb_ref)):
        out_ref[:, t] = ref[...] - change[t * half : (t + 1) * half].reshape(ref.shape)


def update(total, factor, xs, held):
    chunks, size, width = held[0].shape
    n, sub, rows = xs[0].shape
    xspec = pl.BlockSpec((n, sub, size), lambda i: (0, 0, i))
    pspec = pl.BlockSpec((1, size, width), lambda i: (i, 0, 0))
    whole = pl.BlockSpec(memory_space=pltpu.VMEM)
    return pl.pallas_call(
        update_body,
        out_shape=jax.ShapeDtypeStruct((n, 2, sub, rows), F32),
        grid=(chunks,),
        in_specs=[whole, whole, xspec, xspec, pspec, pspec],
        out_specs=pl.BlockSpec((n, 2, sub, size), lambda i: (0, 0, 0, i)),
        scratch_shapes=[pltpu.VMEM((2, 2, width, width), jnp.bfloat16)],
        compiler_params=pltpu.CompilerParams(vmem_limit_bytes=VMEM),
        name="update",
    )(total, factor, *xs, *held)


def shards(eigvecs, reflectors, factors, owner):
    groups = lax.axis_size("row")
    own_count = eigvecs.shape[1]
    rows_here = eigvecs.shape[2] // groups
    width = factors.shape[1]
    split_vecs = eigvecs.reshape(2, own_count // 2, groups, rows_here).transpose(0, 2, 1, 3)
    xs = [lax.all_to_all(split_vecs[t], "row", split_axis=0, concat_axis=0, tiled=True) for t in range(2)]

    me = lax.axis_index("col")
    kept = jnp.stack([jnp.where(me == owner[b], factors[0], 0.0) for b in (1, 0)])
    factor = lax.psum(kept, "col")

    size = rows_here // (GROUPS * CHUNKS)
    plans = jnp.stack([plan(owner[b], step) for b, step in zip((1, 0), STEPS)])
    heads = []
    for block in (1, 0):
        rows = lax.axis_index("row") * rows_here + lax.broadcasted_iota(jnp.int32, (size, width), 0)
        cols = lax.broadcasted_iota(jnp.int32, (size, width), 1) + block * width
        head = jnp.where(rows > cols, reflectors[0, :size], 0.0)
        heads.append(jnp.where(rows == cols, 1.0, head))
    held = [jnp.zeros((GROUPS * CHUNKS, size, width), F32) for _ in range(2)]
    held = lax.optimization_barrier(held)
    got = [None] * GROUPS
    crossed = [None] * GROUPS
    turns = [ring_pairs(step) for step in STEPS]
    for s in range(SLOTS + 1):
        for g in range(GROUPS):
            held, send, across = slot_call(s, g, plans, reflectors, heads, got[g], crossed[g], held)
            if send is not None:
                got[g] = [lax.ppermute(x, "col", turn) for x, turn in zip(send, turns)]
            if across is not None:
                crossed[g] = [lax.ppermute(x, "col", SWAP) for x in across]

    stack = project(xs, held).reshape(groups, 3 * width // groups, width)
    cut = jnp.sum(lax.all_to_all(stack, "row", split_axis=0, concat_axis=0, tiled=True), 0)
    total = lax.all_gather(cut, "row", axis=0, tiled=True).reshape(3, width, width)
    return update(total, factor, xs, held).reshape(1, own_count * groups, rows_here)


def solution(mesh):
    in_specs = (P("col", "row", None), P("col", "row", None), P("col", None, None), P())
    out_specs = P("col", None, "row")
    return jax.shard_map(shards, mesh=mesh, in_specs=in_specs, out_specs=out_specs, check_vma=False)
```

```python
import functools

import jax
import jax.numpy as jnp
from jax import lax
from jax.experimental import pallas as pl
from jax.experimental.pallas import tpu as pltpu
from jax.sharding import PartitionSpec as P

RING = 4
GROUPS = 2
QUARTER = 3
CHUNKS = RING * QUARTER
SLOTS = max(CHUNKS + 2, 3 * QUARTER + 5)
STEPS = (1, -1)
BLOCKS = (1, 0)
MOVES = ((0, 1), (10, 0))
TILE = 512
VMEM = 48 * 2**20
GRANT = 50 * 2**20
F32 = jnp.float32
ANY = pl.BlockSpec(memory_space=pl.ANY)
HBM = pl.BlockSpec(memory_space=pltpu.HBM)
SMEM = pl.BlockSpec(memory_space=pltpu.SMEM)


def ring_pairs(step):
    return [(h * RING + z, h * RING + (z + step) % RING) for h in range(2) for z in range(RING)]


SWAP = [(i, (i + RING) % (2 * RING)) for i in range(2 * RING)]


def chunk_rows(part):
    return -(-part // (CHUNKS * 8)) * 8


def crossing_id(batch, place):
    return jnp.where(place == 0, 3 * QUARTER + batch, 3 * batch + 3 - place)


def cross_slots(s):
    send = next((b for b in range(QUARTER) if s == 3 * b + 3), None)
    inject = next((b for b in range(QUARTER) if s == 3 * b + 5), None)
    return send, inject


def plan(s, owner, step):
    me = lax.axis_index("col")
    far = me // RING != owner // RING
    place = jnp.bitwise_and(step * (me - owner), RING - 1)
    source = me == owner
    _, inject = cross_slots(s)
    index = s - place
    keep = (index >= 0) & (index < CHUNKS) & ~far
    if s == 0:
        keep = source
    for b in range(QUARTER):
        j = s - 1 - (3 * b + 5)
        if 0 <= j < 3:
            index = jnp.where(far, crossing_id(b, jnp.bitwise_and(place - 1 - j, RING - 1)), index)
            keep = keep | far
    index = jnp.clip(index, 0, CHUNKS - 1)
    cross = crossing_id(inject, place) if inject is not None else 0
    return source, index, keep, far, cross


def slot_body(s, group, n_deps, owner_ref, own_ref, *refs):
    refs = list(refs)
    over, inject = cross_slots(s)
    first = s == 0 and group == 0
    none = [None, None]
    heads = [refs.pop(0), refs.pop(0)] if group == 0 else none
    got = [refs.pop(0), refs.pop(0)] if s else none
    crossed = [refs.pop(0), refs.pop(0)] if inject is not None else none
    del refs[: n_deps + (0 if first else 2)]
    held = [refs.pop(0), refs.pop(0)]
    send = [refs.pop(0), refs.pop(0)] if s < SLOTS else none
    across = [refs.pop(0), refs.pop(0)] if over is not None else none
    sems = refs.pop(0)
    part = own_ref.shape[1] // GROUPS
    size = chunk_rows(part)

    now, then = [], []
    for i in range(2):
        source, index, keep, far, cross = plan(s, owner_ref[BLOCKS[i]], STEPS[i])

        def own(c):
            start = min(c * size, part - size)
            if group == 0 and start + size <= heads[i].shape[0]:
                return heads[i].at[pl.ds(start, size)]
            return own_ref.at[0, pl.ds(group * part + start, size)]

        def slot(index):
            start = group * part + jnp.minimum(index * size, part - size)
            return held[i].at[pl.ds(pl.multiple_of(start, 8), size)]

        if s == 0:
            now.append((True, own(0), send[i]))
        elif s < CHUNKS:
            now.append((source, own(s), send[i]))
        passes = ~source if 0 < s < CHUNKS else True
        if inject is not None:
            now.append((far, crossed[i], send[i]))
            now.append((far, crossed[i], slot(cross)))
            passes = ~far if passes is True else passes & ~far
        if 0 < s < SLOTS:
            now.append((passes, got[i], send[i]))
        if s < CHUNKS:
            then.append((source, send[i], slot(s)))
        if s:
            now.append((keep & ~source, got[i], slot(index)))
        if over is not None:
            now.append((source, own(3 * QUARTER + over), across[i]))
            now.append((~source, got[i], across[i]))

    for copies in (now, then):
        for wait in (False, True):
            for n, (when, src, dst) in enumerate(copies):
                copy = pltpu.make_async_copy(src, dst, sems.at[n])
                act = copy.wait if wait else copy.start
                act() if when is True else pl.when(when)(act)


def slot_call(s, group, owner, own, heads, got, crossed, held, deps):
    part, width = own.shape[1] // GROUPS, own.shape[2]
    size = chunk_rows(part)
    chunk = jax.ShapeDtypeStruct((size, width), own.dtype)
    over, inject = cross_slots(s)
    ins, specs = [owner, own], [SMEM, HBM]

    def add(arrays, spec):
        ins.extend(arrays)
        specs.extend([spec] * len(arrays))

    if group == 0:
        add(heads, ANY)
    if s:
        add(got, ANY)
    if inject is not None:
        add(crossed, ANY)
    add(deps, ANY)
    first = len(ins)
    if held is not None:
        add(held, HBM)
    outs = [jax.ShapeDtypeStruct(own.shape[1:], own.dtype)] * 2
    if s < SLOTS:
        outs += [chunk] * 2
    if over is not None:
        outs += [chunk] * 2
    out = pl.pallas_call(
        functools.partial(slot_body, s, group, len(deps)),
        out_shape=outs,
        in_specs=specs,
        out_specs=[HBM] * 2 + [ANY] * (len(outs) - 2),
        scratch_shapes=[pltpu.SemaphoreType.DMA((16,))],
        input_output_aliases={} if held is None else {first: 0, first + 1: 1},
        compiler_params=pltpu.CompilerParams(vmem_limit_bytes=GRANT),
        cost_estimate=pl.CostEstimate(flops=0, bytes_accessed=4 * 2**20, transcendentals=0),
        name=f"slot{s}_{group}",
    )(*ins)
    held, out = out[:2], out[2:]
    send = across = None
    if s < SLOTS:
        send, out = out[:2], out[2:]
    if over is not None:
        across = out
    return held, send, across


def regroup_body(first, groups, x_ref, dep_ref, out_ref, room, sems):
    rows = out_ref.shape[2]

    def come(j):
        src = x_ref.at[0, pl.ds(first, out_ref.shape[1]), pl.ds(j * rows, rows)]
        return pltpu.make_async_copy(src, room.at[j], sems.at[0, j])

    def leave(j):
        return pltpu.make_async_copy(room.at[j], out_ref.at[j], sems.at[1, j])

    for j in range(groups):
        come(j).start()
    for j in range(groups):
        come(j).wait()
        leave(j).start()
    for j in range(groups):
        leave(j).wait()


def regroup(x, first, count, groups, dep):
    shape = (groups, count, x.shape[2] // groups)
    return pl.pallas_call(
        functools.partial(regroup_body, first, groups),
        out_shape=jax.ShapeDtypeStruct(shape, x.dtype),
        in_specs=[HBM, ANY],
        out_specs=HBM,
        scratch_shapes=[pltpu.VMEM(shape, x.dtype), pltpu.SemaphoreType.DMA((2, groups))],
        compiler_params=pltpu.CompilerParams(vmem_limit_bytes=GRANT),
        name="regroup",
    )(x, dep)


def parts_of(x):
    high = x.astype(jnp.bfloat16)
    low = (x - high.astype(F32)).astype(jnp.bfloat16)
    return high, low


def dot3(left, right, dims):
    (lh, ll), (rh, rl) = left, right
    go = functools.partial(lax.dot_general, dimension_numbers=(dims, ((), ())), preferred_element_type=F32)
    return go(lh, rh) + (go(lh, rl) + go(ll, rh))


def full(left, right, dims):
    return lax.dot_general(
        left, right, (dims, ((), ())), precision=lax.Precision.HIGHEST, preferred_element_type=F32
    )


def project_body(xa_ref, xb_ref, p1_ref, p0_ref, out_ref):
    half = xa_ref.shape[0]
    p1, p0 = parts_of(p1_ref[...]), parts_of(p0_ref[...])

    @pl.when(pl.program_id(0) == 0)
    def _():
        out_ref[...] = jnp.zeros_like(out_ref)

    for t, ref in enumerate((xa_ref, xb_ref)):
        x = parts_of(ref[...])
        at = pl.ds(t * half, half)
        out_ref[0, at] += dot3(x, p1, ((1,), (0,)))
        out_ref[1, at] += dot3(x, p0, ((1,), (0,)))
    out_ref[2] += dot3(p1, p0, ((0,), (0,)))


def project(fields, held):
    rows, width = held[0].shape
    xspec = pl.BlockSpec((fields[0].shape[0], TILE), lambda i: (0, i))
    pspec = pl.BlockSpec((TILE, width), lambda i: (i, 0))
    return pl.pallas_call(
        project_body,
        out_shape=jax.ShapeDtypeStruct((3, width, width), F32),
        grid=(rows // TILE,),
        in_specs=[xspec, xspec, pspec, pspec],
        out_specs=pl.BlockSpec((3, width, width), lambda i: (0, 0, 0)),
        compiler_params=pltpu.CompilerParams(vmem_limit_bytes=VMEM),
        name="project",
    )(*fields, *held)


def update_body(sum_ref, f1_ref, f0_ref, xa_ref, xb_ref, p1_ref, p0_ref, out_ref, y_ref):
    @pl.when(pl.program_id(0) == 0)
    def _():
        y1 = full(sum_ref[0], f1_ref[...], ((1,), (1,)))
        w0 = sum_ref[1] - full(y1, sum_ref[2], ((1,), (0,)))
        y0 = full(w0, f0_ref[...], ((1,), (1,)))
        for i, y in enumerate((y1, y0)):
            high, low = parts_of(y)
            y_ref[i, 0] = high
            y_ref[i, 1] = low

    change = 0
    for i, ref in enumerate((p1_ref, p0_ref)):
        change += dot3((y_ref[i, 0], y_ref[i, 1]), parts_of(ref[...]), ((1,), (1,)))
    n, _, sub, rows = out_ref.shape
    for t, ref in enumerate((xa_ref, xb_ref)):
        half = ref.shape[0]
        out_ref[:, t] = (ref[...] - change[t * half : (t + 1) * half]).reshape(n, sub, rows)


def update(total, factors, fields, held, groups):
    rows, width = held[0].shape
    half = fields[0].shape[0]
    xspec = pl.BlockSpec((half, TILE), lambda i: (0, i))
    pspec = pl.BlockSpec((TILE, width), lambda i: (i, 0))
    whole = pl.BlockSpec(memory_space=pltpu.VMEM)
    return pl.pallas_call(
        update_body,
        out_shape=jax.ShapeDtypeStruct((groups, 2, half // groups, rows), F32),
        grid=(rows // TILE,),
        in_specs=[whole, whole, whole, xspec, xspec, pspec, pspec],
        out_specs=pl.BlockSpec((groups, 2, half // groups, TILE), lambda i: (0, 0, 0, i)),
        scratch_shapes=[pltpu.VMEM((2, 2, width, width), jnp.bfloat16)],
        compiler_params=pltpu.CompilerParams(vmem_limit_bytes=VMEM),
        name="update",
    )(total, *factors, *fields, *held)


def shared_factors(factor, owner):
    second = lax.axis_index("row") % 2 == 1
    mine = jnp.where(lax.axis_index("col") == jnp.where(second, owner[0], owner[1]), factor, 0.0)
    for pairs in (ring_pairs(1), ring_pairs(2), SWAP):
        mine = mine + lax.ppermute(mine, "col", pairs)
    other = lax.ppermute(mine, "row", [(i, i ^ 1) for i in range(lax.axis_size("row"))])
    return [jnp.where(second, other, mine), jnp.where(second, mine, other)]


def shards(eigvecs, reflectors, factors, owner):
    groups = lax.axis_size("row")
    own_count = eigvecs.shape[1]
    rows_here = eigvecs.shape[2] // groups
    width = factors.shape[2]
    used = shared_factors(factors[0], owner)

    size = chunk_rows(rows_here // GROUPS)
    top = -(-2 * width // size) * size
    heads = []
    for block in BLOCKS:
        rows = lax.axis_index("row") * rows_here + lax.broadcasted_iota(jnp.int32, (top, width), 0)
        cols = lax.broadcasted_iota(jnp.int32, (top, width), 1) + block * width
        head = jnp.where(rows > cols, reflectors[0, :top], 0.0)
        heads.append(jnp.where(rows == cols, 1.0, head))
    held = None
    got = [None] * GROUPS
    crossed = [None] * GROUPS
    turns = [ring_pairs(step) for step in STEPS]
    fields = []
    deps = {}
    for s in range(SLOTS + 1):
        for g in range(GROUPS):
            held, send, across = slot_call(
                s, g, owner, reflectors, heads, got[g], crossed[g], held, deps.get((s, g), [])
            )
            if send is not None:
                got[g] = [lax.ppermute(x, "col", turn) for x, turn in zip(send, turns)]
            if across is not None:
                crossed[g] = [lax.ppermute(x, "col", SWAP) for x in across]
            if (s, g) in MOVES:
                half = own_count // 2
                split = regroup(eigvecs, len(fields) * half, half, groups, send[0])
                moved = lax.all_to_all(split, "row", split_axis=0, concat_axis=0, tiled=True)
                fields.append(moved.reshape(groups * half, rows_here))
                if len(fields) == 1:
                    deps = {(1, 0): [split], (6, 0): [fields[0]], (11, 1): used}

    stack = project(fields, held).reshape(groups, 3 * width // groups, width)
    cut = jnp.sum(lax.all_to_all(stack, "row", split_axis=0, concat_axis=0, tiled=True), 0)
    total = lax.all_gather(cut, "row", axis=0, tiled=True).reshape(3, width, width)
    out = update(total, used, fields, held, groups)
    return out.reshape(1, own_count * groups, rows_here)


def solution(mesh):
    in_specs = (P("col", "row", None), P("col", "row", None), P("col", None, None), P())
    out_specs = P("col", None, "row")
    return jax.shard_map(shards, mesh=mesh, in_specs=in_specs, out_specs=out_specs, check_vma=False)
```

```python
import functools

import jax
import jax.numpy as jnp
from jax import lax
from jax.experimental import pallas as pl
from jax.experimental.pallas import tpu as pltpu
from jax.sharding import PartitionSpec as P

RING = 4
GROUPS = 2
QUARTER = 3
CHUNKS = RING * QUARTER
SLOTS = max(CHUNKS + 2, 3 * QUARTER + 5)
STEPS = (1, -1)
BLOCKS = (1, 0)
SECOND = (11, 1)
TILE = 2048
VMEM = 48 * 2**20
GRANT = 50 * 2**20
F32 = jnp.float32
ANY = pl.BlockSpec(memory_space=pl.ANY)
HBM = pl.BlockSpec(memory_space=pltpu.HBM)
SMEM = pl.BlockSpec(memory_space=pltpu.SMEM)


def ring_pairs(step):
    return [(h * RING + z, h * RING + (z + step) % RING) for h in range(2) for z in range(RING)]


SWAP = [(i, (i + RING) % (2 * RING)) for i in range(2 * RING)]


def sizes(own, factor):
    part, extra = own.shape[1] // GROUPS, factor.shape[1] // GROUPS
    assert (part + extra) % (CHUNKS * 8) == 0
    return part, extra, (part + extra) // CHUNKS


def crossing_id(batch, place):
    return jnp.where(place == 0, 3 * QUARTER + batch, 3 * batch + 3 - place)


def cross_slots(s):
    send = next((b for b in range(QUARTER) if s == 3 * b + 3), None)
    inject = next((b for b in range(QUARTER) if s == 3 * b + 5), None)
    return send, inject


def plan(s, owner, step):
    me = lax.axis_index("col")
    far = me // RING != owner // RING
    place = jnp.bitwise_and(step * (me - owner), RING - 1)
    source = me == owner
    _, inject = cross_slots(s)
    index = s - place
    keep = (index >= 0) & (index < CHUNKS) & ~far
    if s == 0:
        keep = source
    for b in range(QUARTER):
        j = s - 1 - (3 * b + 5)
        if 0 <= j < 3:
            index = jnp.where(far, crossing_id(b, jnp.bitwise_and(place - 1 - j, RING - 1)), index)
            keep = keep | far
    index = jnp.clip(index, 0, CHUNKS - 1)
    cross = crossing_id(inject, place) if inject is not None else 0
    return source, index, keep, far, cross


def slot_body(s, group, carried, owner_ref, own_ref, factor_ref, *refs):
    refs = list(refs)
    over, inject = cross_slots(s)
    first = s == 0 and group == 0
    none = [None, None]
    heads = [refs.pop(0), refs.pop(0)] if group == 0 else none
    got = [refs.pop(0), refs.pop(0)] if s else none
    crossed = refs.pop(0) if inject is not None else None
    del refs[: carried + (0 if first else 2)]
    held = [refs.pop(0), refs.pop(0)]
    send = [refs.pop(0), refs.pop(0)] if s < SLOTS else none
    across = refs.pop(0) if over is not None else None
    del refs[: len(refs) - 2]
    stage, sems = refs
    part, extra, size = sizes(own_ref, factor_ref)

    now, then = [], []
    for i in range(2):
        source, index, keep, far, cross = plan(s, owner_ref[BLOCKS[i]], STEPS[i])
        both = pl.ds(i * size, size)

        def bring(when, c, to):
            start, stop = c * size, min((c + 1) * size, part)
            if group == 0 and stop <= heads[i].shape[0]:
                now.append((when, heads[i].at[pl.ds(start, size)], to))
                return
            src = own_ref.at[0, pl.ds(group * part + start, stop - start)]
            now.append((when, src, to.at[pl.ds(0, stop - start)]))
            if stop - start < size:
                src = factor_ref.at[0, pl.ds(group * extra, extra)]
                now.append((when, src, to.at[pl.ds(stop - start, extra)]))

        def slot(index):
            return held[i].at[group, pl.ds(pl.multiple_of(index * size, 8), size)]

        here, there = stage.at[i, 0], stage.at[i, 1]
        if s < CHUNKS:
            when = True if s == 0 else source
            bring(when, s, here)
            then.append((when, here, send[i]))
            then.append((source, here, slot(s)))
        passes = ~source if 0 < s < CHUNKS else True
        if inject is not None:
            now.append((far, crossed.at[both], send[i]))
            now.append((far, crossed.at[both], slot(cross)))
            passes = ~far if passes is True else passes & ~far
        if 0 < s < SLOTS:
            now.append((passes, got[i], send[i]))
        if s:
            now.append((keep & ~source, got[i], slot(index)))
        if over is not None:
            bring(source, 3 * QUARTER + over, there)
            then.append((source, there, across.at[both]))
            now.append((~source, got[i], across.at[both]))

    for copies in (now, then):
        for wait in (False, True):
            for n, (when, src, dst) in enumerate(copies):
                copy = pltpu.make_async_copy(src, dst, sems.at[n])
                act = copy.wait if wait else copy.start
                act() if when is True else pl.when(when)(act)


def slot_call(s, group, owner, own, factor, heads, got, crossed, held, wanted=(), carried=None):
    width = own.shape[2]
    part, extra, size = sizes(own, factor)
    over, inject = cross_slots(s)
    ins, specs = [owner, own, factor], [SMEM, HBM, HBM]
    outs, out_specs = [jax.ShapeDtypeStruct((GROUPS, part + extra, width), own.dtype)] * 2, [HBM] * 2
    aliases = {}

    def add(arrays, spec):
        ins.extend(arrays)
        specs.extend([spec] * len(arrays))

    if group == 0:
        add(heads, ANY)
    if s:
        add(got, ANY)
    if inject is not None:
        add([crossed], ANY)
    add(wanted, ANY)
    if carried is not None:
        add([carried], HBM)
    if held is not None:
        aliases = {len(ins): 0, len(ins) + 1: 1}
        add(held, HBM)
    if s < SLOTS:
        outs += [jax.ShapeDtypeStruct((size, width), own.dtype)] * 2
    if over is not None:
        outs += [jax.ShapeDtypeStruct((2 * size, width), own.dtype)]
    out_specs += [ANY] * (len(outs) - 2)
    if carried is not None:
        aliases[len(ins) - 3] = len(outs)
        outs += [jax.ShapeDtypeStruct(carried.shape, carried.dtype)]
        out_specs += [HBM]
    out = pl.pallas_call(
        functools.partial(slot_body, s, group, len(wanted) + (carried is not None)),
        out_shape=outs,
        in_specs=specs,
        out_specs=out_specs,
        scratch_shapes=[pltpu.VMEM((2, 2, size, width), own.dtype), pltpu.SemaphoreType.DMA((20,))],
        input_output_aliases=aliases,
        compiler_params=pltpu.CompilerParams(vmem_limit_bytes=GRANT),
        cost_estimate=pl.CostEstimate(flops=0, bytes_accessed=4 * 2**20, transcendentals=0),
        name=f"slot{s}_{group}",
    )(*ins)
    out = list(out)
    held, out = out[:2], out[2:]
    send = [out.pop(0), out.pop(0)] if s < SLOTS else None
    across = out.pop(0) if over is not None else None
    return held, send, across, out.pop(0) if out else None


def regroup_body(first, groups, x_ref, dep_ref, out_ref, room, sems):
    rows = out_ref.shape[2]

    def come(j):
        src = x_ref.at[0, pl.ds(first, out_ref.shape[1]), pl.ds(j * rows, rows)]
        return pltpu.make_async_copy(src, room.at[j], sems.at[0, j])

    def leave(j):
        return pltpu.make_async_copy(room.at[j], out_ref.at[j], sems.at[1, j])

    for j in range(groups):
        come(j).start()
    for j in range(groups):
        come(j).wait()
        leave(j).start()
    for j in range(groups):
        leave(j).wait()


def regroup(x, first, count, groups, dep):
    shape = (groups, count, x.shape[2] // groups)
    return pl.pallas_call(
        functools.partial(regroup_body, first, groups),
        out_shape=jax.ShapeDtypeStruct(shape, x.dtype),
        in_specs=[HBM, ANY],
        out_specs=HBM,
        scratch_shapes=[pltpu.VMEM(shape, x.dtype), pltpu.SemaphoreType.DMA((2, groups))],
        compiler_params=pltpu.CompilerParams(vmem_limit_bytes=GRANT),
        name="regroup",
    )(x, dep)


def parts_of(x):
    high = x.astype(jnp.bfloat16)
    low = (x - high.astype(F32)).astype(jnp.bfloat16)
    return high, low


def dot3(left, right, dims):
    (lh, ll), (rh, rl) = left, right
    go = functools.partial(lax.dot_general, dimension_numbers=(dims, ((), ())), preferred_element_type=F32)
    return go(lh, rh) + (go(lh, rl) + go(ll, rh))


def full(left, right, dims):
    return lax.dot_general(
        left, right, (dims, ((), ())), precision=lax.Precision.HIGHEST, preferred_element_type=F32
    )


def project_first_body(x_ref, p1_ref, p0_ref, w_ref, gram_ref):
    x, p1, p0 = parts_of(x_ref[...]), parts_of(p1_ref[0]), parts_of(p0_ref[0])

    @pl.when(pl.program_id(0) == 0)
    def _():
        w_ref[...] = jnp.zeros_like(w_ref)
        gram_ref[...] = jnp.zeros_like(gram_ref)

    w_ref[0] += dot3(x, p1, ((1,), (0,)))
    w_ref[1] += dot3(x, p0, ((1,), (0,)))
    gram_ref[...] += dot3(p1, p0, ((0,), (0,)))


def project_second_body(x_ref, p1_ref, p0_ref, first_ref, gram_ref, mine_ref, other_ref, w_ref, sum_ref):
    x, p1, p0 = parts_of(x_ref[...]), parts_of(p1_ref[0]), parts_of(p0_ref[0])

    @pl.when(pl.program_id(0) == 0)
    def _():
        w_ref[...] = jnp.zeros_like(w_ref)

    w_ref[0] += dot3(x, p1, ((1,), (0,)))
    w_ref[1] += dot3(x, p0, ((1,), (0,)))

    @pl.when(pl.program_id(0) == pl.num_programs(0) - 1)
    def _():
        half, width = w_ref.shape[1:]
        for i in range(2):
            sum_ref[pl.ds(2 * i * half, half)] = first_ref[i]
            sum_ref[pl.ds((2 * i + 1) * half, half)] = w_ref[i]
        sum_ref[pl.ds(4 * half, width)] = gram_ref[...]
        core = lax.axis_index("row") % 2
        rows = mine_ref.shape[0]
        mine_ref[...] = sum_ref[pl.ds(pl.multiple_of(core * rows, 8), rows)]
        other_ref[...] = sum_ref[pl.ds(pl.multiple_of((1 - core) * rows, 8), rows)]


def project(fields, held):
    width = held[0].shape[2]
    half, rows = fields[0].shape
    tiles = rows // GROUPS // TILE
    xspec = pl.BlockSpec((half, TILE), lambda i: (0, i))
    pspec = pl.BlockSpec((1, TILE, width), lambda i: (i // tiles, i % tiles, 0))
    whole = pl.BlockSpec(memory_space=pltpu.VMEM)
    w_shape = jax.ShapeDtypeStruct((2, half, width), F32)
    params = pltpu.CompilerParams(vmem_limit_bytes=VMEM)
    first = pl.pallas_call(
        project_first_body,
        out_shape=[w_shape, jax.ShapeDtypeStruct((width, width), F32)],
        grid=(rows // TILE,),
        in_specs=[xspec, pspec, pspec],
        out_specs=[pl.BlockSpec((2, half, width), lambda i: (0, 0, 0)), pl.BlockSpec((width, width), lambda i: (0, 0))],
        compiler_params=params,
        cost_estimate=pl.CostEstimate(flops=6 * rows * width * 2 * width, bytes_accessed=20 * 2**20, transcendentals=0),
        name="project_first",
    )(fields[0], *held)
    count = (4 * half + width) // 2
    return pl.pallas_call(
        project_second_body,
        out_shape=[jax.ShapeDtypeStruct((count, width), F32)] * 2,
        grid=(rows // TILE,),
        in_specs=[xspec, pspec, pspec, whole, whole],
        out_specs=[pl.BlockSpec((count, width), lambda i: (0, 0))] * 2,
        scratch_shapes=[pltpu.VMEM((2, half, width), F32), pltpu.VMEM((2 * count, width), F32)],
        compiler_params=params,
        cost_estimate=pl.CostEstimate(flops=6 * rows * width * width, bytes_accessed=20 * 2**20, transcendentals=0),
        name="project_second",
    )(fields[1], *held, *first)


def row_sum(mine, other):
    devices = lax.axis_size("row")
    pairs = [(i, i ^ 1) for i in range(devices)]
    alike = [[i for i in range(devices) if i % 2 == core] for core in range(2)]
    swap = functools.partial(lax.all_to_all, axis_name="row", split_axis=0, concat_axis=0, tiled=True, axis_index_groups=alike)
    count, width = mine.shape
    chips = devices // 2
    mine = mine + lax.ppermute(other, "row", pairs)
    piece = jnp.sum(swap(mine.reshape(chips, count // chips, width)), 0)
    mine = swap(jnp.broadcast_to(piece, (chips, *piece.shape))).reshape(count, width)
    return mine, lax.ppermute(mine, "row", pairs)


def update_body(mine_ref, other_ref, f1_ref, f0_ref, xa_ref, xb_ref, p1_ref, p0_ref, out_ref, sum_ref, y_ref):
    width = p1_ref.shape[2]

    @pl.when(pl.program_id(0) == 0)
    def _():
        core = lax.axis_index("row") % 2
        rows = mine_ref.shape[0]
        sum_ref[pl.ds(pl.multiple_of(core * rows, 8), rows)] = mine_ref[...]
        sum_ref[pl.ds(pl.multiple_of((1 - core) * rows, 8), rows)] = other_ref[...]
        w1, w0, gram = (sum_ref[pl.ds(i * width, width)] for i in range(3))
        y1 = full(w1, f1_ref[...].reshape(width, width), ((1,), (1,)))
        w0 = w0 - full(y1, gram, ((1,), (0,)))
        y0 = full(w0, f0_ref[...].reshape(width, width), ((1,), (1,)))
        for i, y in enumerate((y1, y0)):
            high, low = parts_of(y)
            y_ref[i, 0] = high
            y_ref[i, 1] = low

    change = 0
    for i, ref in enumerate((p1_ref, p0_ref)):
        change += dot3((y_ref[i, 0], y_ref[i, 1]), parts_of(ref[0]), ((1,), (1,)))
    n, _, sub, rows = out_ref.shape
    for t, ref in enumerate((xa_ref, xb_ref)):
        half = ref.shape[0]
        out_ref[:, t] = (ref[...] - change[t * half : (t + 1) * half]).reshape(n, sub, rows)


def update(mine, other, fields, held, groups):
    width = held[0].shape[2]
    half, rows = fields[0].shape
    tiles = rows // GROUPS // TILE
    xspec = pl.BlockSpec((half, TILE), lambda i: (0, i))
    pspec = pl.BlockSpec((1, TILE, width), lambda i: (i // tiles, i % tiles, 0))
    extra = width // GROUPS
    fspec = pl.BlockSpec((GROUPS, extra, width), lambda i: (0, rows // GROUPS // extra, 0))
    whole = pl.BlockSpec(memory_space=pltpu.VMEM)
    return pl.pallas_call(
        update_body,
        out_shape=jax.ShapeDtypeStruct((groups, 2, half // groups, rows), F32),
        grid=(rows // TILE,),
        in_specs=[whole, whole, fspec, fspec, xspec, xspec, pspec, pspec],
        out_specs=pl.BlockSpec((groups, 2, half // groups, TILE), lambda i: (0, 0, 0, i)),
        scratch_shapes=[
            pltpu.VMEM((2 * mine.shape[0], width), F32),
            pltpu.VMEM((2, 2, width, width), jnp.bfloat16),
        ],
        compiler_params=pltpu.CompilerParams(vmem_limit_bytes=VMEM),
        name="update",
    )(mine, other, *held, *fields, *held)


def shards(eigvecs, reflectors, factors, owner):
    groups = lax.axis_size("row")
    own_count = eigvecs.shape[1]
    rows_here = eigvecs.shape[2] // groups
    width = factors.shape[2]
    half = own_count // 2

    size = sizes(reflectors, factors)[2]
    top = -(-2 * width // size) * size
    heads = []
    for block in BLOCKS:
        rows = lax.axis_index("row") * rows_here + lax.broadcasted_iota(jnp.int32, (top, width), 0)
        cols = lax.broadcasted_iota(jnp.int32, (top, width), 1) + block * width
        head = jnp.where(rows > cols, reflectors[0, :top], 0.0)
        heads.append(jnp.where(rows == cols, 1.0, head))
    held = None
    got = [None] * GROUPS
    crossed = [None] * GROUPS
    turns = [ring_pairs(step) for step in STEPS]
    swap = functools.partial(lax.all_to_all, axis_name="row", split_axis=0, concat_axis=0, tiled=True)
    fields = []
    splits = []
    wanted = {}
    for s in range(SLOTS + 1):
        for g in range(GROUPS):
            held, send, across, carried = slot_call(
                s, g, owner, reflectors, factors, heads, got[g], crossed[g], held,
                wanted.get((s, g), []), splits[1] if (s, g) == SECOND else None,
            )
            if send is not None:
                got[g] = [lax.ppermute(x, "col", turn) for x, turn in zip(send, turns)]
            if across is not None:
                crossed[g] = lax.ppermute(across, "col", SWAP)
            if (s, g) in ((0, GROUPS - 1), (1, GROUPS - 1)):
                splits.append(regroup(eigvecs, len(splits) * half, half, groups, send[0]))
                wanted[s + 1, 0] = [splits[-1]]
            if len(splits) == 1 and not fields:
                fields.append(swap(splits[0]).reshape(groups * half, rows_here))
                wanted[6, 0] = [fields[0]]
            if carried is not None:
                fields.append(swap(carried).reshape(groups * half, rows_here))

    mine, other = row_sum(*project(fields, held))
    return update(mine, other, fields, held, groups).reshape(1, own_count * groups, rows_here)


def solution(mesh):
    in_specs = (P("col", "row", None), P("col", "row", None), P("col", None, None), P())
    out_specs = P("col", None, "row")
    return jax.shard_map(shards, mesh=mesh, in_specs=in_specs, out_specs=out_specs, check_vma=False)
```

```python
import functools

import jax
import jax.numpy as jnp
from jax import lax
from jax.experimental import pallas as pl
from jax.experimental.pallas import tpu as pltpu
from jax.sharding import PartitionSpec as P

RING = 4
GROUPS = 2
QUARTER = 3
CHUNKS = RING * QUARTER
SLOTS = max(CHUNKS + 2, 3 * QUARTER + 5)
STEPS = (1, -1)
BLOCKS = (1, 0)
SECOND = (11, 1)
TILE = 2048
VMEM = 48 * 2**20
GRANT = 50 * 2**20
F32 = jnp.float32
ANY = pl.BlockSpec(memory_space=pl.ANY)
HBM = pl.BlockSpec(memory_space=pltpu.HBM)
SMEM = pl.BlockSpec(memory_space=pltpu.SMEM)


def ring_pairs(step):
    return [(h * RING + z, h * RING + (z + step) % RING) for h in range(2) for z in range(RING)]


SWAP = [(i, (i + RING) % (2 * RING)) for i in range(2 * RING)]


def sizes(own, factor):
    part, extra = own.shape[1] // GROUPS, factor.shape[1] // GROUPS
    assert (part + extra) % (CHUNKS * 8) == 0
    return part, extra, (part + extra) // CHUNKS


def crossing_id(batch, place):
    return jnp.where(place == 0, 3 * QUARTER + batch, 3 * batch + 3 - place)


def cross_slots(s):
    send = next((b for b in range(QUARTER) if s == 3 * b + 3), None)
    inject = next((b for b in range(QUARTER) if s == 3 * b + 5), None)
    return send, inject


def plan(s, owner, step):
    me = lax.axis_index("col")
    far = me // RING != owner // RING
    place = jnp.bitwise_and(step * (me - owner), RING - 1)
    source = me == owner
    _, inject = cross_slots(s)
    index = s - place
    keep = (index >= 0) & (index < CHUNKS) & ~far
    if s == 0:
        keep = source
    for b in range(QUARTER):
        j = s - 1 - (3 * b + 5)
        if 0 <= j < 3:
            index = jnp.where(far, crossing_id(b, jnp.bitwise_and(place - 1 - j, RING - 1)), index)
            keep = keep | far
    index = jnp.clip(index, 0, CHUNKS - 1)
    cross = crossing_id(inject, place) if inject is not None else 0
    return source, index, keep, far, cross


def slot_body(s, group, carried, owner_ref, own_ref, factor_ref, *refs):
    refs = list(refs)
    over, inject = cross_slots(s)
    first = s == 0 and group == 0
    none = [None, None]
    heads = [refs.pop(0), refs.pop(0)] if group == 0 else none
    got = [refs.pop(0), refs.pop(0)] if s else none
    crossed = refs.pop(0) if inject is not None else None
    del refs[: carried + (0 if first else 2)]
    held = [refs.pop(0), refs.pop(0)]
    send = [refs.pop(0), refs.pop(0)] if s < SLOTS else none
    across = refs.pop(0) if over is not None else None
    del refs[: len(refs) - 2]
    stage, sems = refs
    part, extra, size = sizes(own_ref, factor_ref)

    now, then = [], []
    for i in range(2):
        source, index, keep, far, cross = plan(s, owner_ref[BLOCKS[i]], STEPS[i])
        both = pl.ds(i * size, size)

        def bring(when, c, to):
            start, stop = c * size, min((c + 1) * size, part)
            if group == 0 and stop <= heads[i].shape[0]:
                now.append((when, heads[i].at[pl.ds(start, size)], to))
                return
            src = own_ref.at[0, pl.ds(group * part + start, stop - start)]
            now.append((when, src, to.at[pl.ds(0, stop - start)]))
            if stop - start < size:
                src = factor_ref.at[0, pl.ds(group * extra, extra)]
                now.append((when, src, to.at[pl.ds(stop - start, extra)]))

        def slot(index):
            return held[i].at[group, pl.ds(pl.multiple_of(index * size, 8), size)]

        here, there = stage.at[i, 0], stage.at[i, 1]
        if s < CHUNKS:
            when = True if s == 0 else source
            bring(when, s, here)
            then.append((when, here, send[i]))
            then.append((source, here, slot(s)))
        passes = ~source if 0 < s < CHUNKS else True
        if inject is not None:
            now.append((far, crossed.at[both], send[i]))
            now.append((far, crossed.at[both], slot(cross)))
            passes = ~far if passes is True else passes & ~far
        if 0 < s < SLOTS:
            now.append((passes, got[i], send[i]))
        if s:
            now.append((keep & ~source, got[i], slot(index)))
        if over is not None:
            bring(source, 3 * QUARTER + over, there)
            then.append((source, there, across.at[both]))
            now.append((~source, got[i], across.at[both]))

    for copies in (now, then):
        for wait in (False, True):
            for n, (when, src, dst) in enumerate(copies):
                copy = pltpu.make_async_copy(src, dst, sems.at[n])
                act = copy.wait if wait else copy.start
                act() if when is True else pl.when(when)(act)


def slot_call(s, group, owner, own, factor, heads, got, crossed, held, wanted=(), carried=None):
    width = own.shape[2]
    part, extra, size = sizes(own, factor)
    over, inject = cross_slots(s)
    ins, specs = [owner, own, factor], [SMEM, HBM, HBM]
    outs, out_specs = [jax.ShapeDtypeStruct((GROUPS, part + extra, width), own.dtype)] * 2, [HBM] * 2
    aliases = {}

    def add(arrays, spec):
        ins.extend(arrays)
        specs.extend([spec] * len(arrays))

    if group == 0:
        add(heads, ANY)
    if s:
        add(got, ANY)
    if inject is not None:
        add([crossed], ANY)
    add(wanted, ANY)
    if carried is not None:
        add([carried], HBM)
    if held is not None:
        aliases = {len(ins): 0, len(ins) + 1: 1}
        add(held, HBM)
    if s < SLOTS:
        outs += [jax.ShapeDtypeStruct((size, width), own.dtype)] * 2
    if over is not None:
        outs += [jax.ShapeDtypeStruct((2 * size, width), own.dtype)]
    out_specs += [ANY] * (len(outs) - 2)
    if carried is not None:
        aliases[len(ins) - 3] = len(outs)
        outs += [jax.ShapeDtypeStruct(carried.shape, carried.dtype)]
        out_specs += [HBM]
    out = pl.pallas_call(
        functools.partial(slot_body, s, group, len(wanted) + (carried is not None)),
        out_shape=outs,
        in_specs=specs,
        out_specs=out_specs,
        scratch_shapes=[pltpu.VMEM((2, 2, size, width), own.dtype), pltpu.SemaphoreType.DMA((20,))],
        input_output_aliases=aliases,
        compiler_params=pltpu.CompilerParams(vmem_limit_bytes=GRANT),
        cost_estimate=pl.CostEstimate(flops=0, bytes_accessed=4 * 2**20, transcendentals=0),
        name=f"slot{s}_{group}",
    )(*ins)
    out = list(out)
    held, out = out[:2], out[2:]
    send = [out.pop(0), out.pop(0)] if s < SLOTS else None
    across = out.pop(0) if over is not None else None
    return held, send, across, out.pop(0) if out else None


def regroup_body(first, groups, x_ref, dep_ref, out_ref, room, sems):
    rows = out_ref.shape[2]

    def come(j):
        src = x_ref.at[0, pl.ds(first, out_ref.shape[1]), pl.ds(j * rows, rows)]
        return pltpu.make_async_copy(src, room.at[j], sems.at[0, j])

    def leave(j):
        return pltpu.make_async_copy(room.at[j], out_ref.at[j], sems.at[1, j])

    for j in range(groups):
        come(j).start()
    for j in range(groups):
        come(j).wait()
        leave(j).start()
    for j in range(groups):
        leave(j).wait()


def regroup(x, first, count, groups, dep):
    shape = (groups, count, x.shape[2] // groups)
    return pl.pallas_call(
        functools.partial(regroup_body, first, groups),
        out_shape=jax.ShapeDtypeStruct(shape, x.dtype),
        in_specs=[HBM, ANY],
        out_specs=HBM,
        scratch_shapes=[pltpu.VMEM(shape, x.dtype), pltpu.SemaphoreType.DMA((2, groups))],
        compiler_params=pltpu.CompilerParams(vmem_limit_bytes=GRANT),
        name="regroup",
    )(x, dep)


def parts_of(x):
    high = x.astype(jnp.bfloat16)
    low = (x - high.astype(F32)).astype(jnp.bfloat16)
    return high, low


def dot3(left, right, dims):
    (lh, ll), (rh, rl) = left, right
    go = functools.partial(lax.dot_general, dimension_numbers=(dims, ((), ())), preferred_element_type=F32)
    return go(lh, rh) + (go(lh, rl) + go(ll, rh))


def full(left, right, dims):
    return lax.dot_general(
        left, right, (dims, ((), ())), precision=lax.Precision.HIGHEST, preferred_element_type=F32
    )


def project_body(xa_ref, xb_ref, p1_ref, p0_ref, mine_ref, other_ref, sum_ref):
    half, width = xa_ref.shape[0], p1_ref.shape[2]
    p1, p0 = parts_of(p1_ref[0]), parts_of(p0_ref[0])

    @pl.when(pl.program_id(0) == 0)
    def _():
        sum_ref[...] = jnp.zeros_like(sum_ref)

    x = parts_of(jnp.concatenate([xa_ref[...], xb_ref[...]], 0))
    count = 2 * half
    sum_ref[pl.ds(0, count)] += dot3(x, p1, ((1,), (0,)))
    sum_ref[pl.ds(count, count)] += dot3(x, p0, ((1,), (0,)))
    sum_ref[pl.ds(2 * count, width)] += dot3(p1, p0, ((0,), (0,)))

    @pl.when(pl.program_id(0) == pl.num_programs(0) - 1)
    def _():
        core = lax.axis_index("row") % 2
        rows = mine_ref.shape[0]
        mine_ref[...] = sum_ref[pl.ds(pl.multiple_of(core * rows, 8), rows)]
        other_ref[...] = sum_ref[pl.ds(pl.multiple_of((1 - core) * rows, 8), rows)]


def project(fields, held):
    width = held[0].shape[2]
    half, rows = fields[0].shape
    tiles = rows // GROUPS // TILE
    xspec = pl.BlockSpec((half, TILE), lambda i: (0, i))
    pspec = pl.BlockSpec((1, TILE, width), lambda i: (i // tiles, i % tiles, 0))
    count = (4 * half + width) // 2
    return pl.pallas_call(
        project_body,
        out_shape=[jax.ShapeDtypeStruct((count, width), F32)] * 2,
        grid=(rows // TILE,),
        in_specs=[xspec, xspec, pspec, pspec],
        out_specs=[pl.BlockSpec((count, width), lambda i: (0, 0))] * 2,
        scratch_shapes=[pltpu.VMEM((2 * count, width), F32)],
        compiler_params=pltpu.CompilerParams(vmem_limit_bytes=VMEM),
        name="project",
    )(*fields, *held)


def row_sum(mine, other):
    devices = lax.axis_size("row")
    pairs = [(i, i ^ 1) for i in range(devices)]
    alike = [[i for i in range(devices) if i % 2 == core] for core in range(2)]
    swap = functools.partial(lax.all_to_all, axis_name="row", split_axis=0, concat_axis=0, tiled=True, axis_index_groups=alike)
    count, width = mine.shape
    chips = devices // 2
    mine = mine + lax.ppermute(other, "row", pairs)
    piece = jnp.sum(swap(mine.reshape(chips, count // chips, width)), 0)
    mine = swap(jnp.broadcast_to(piece, (chips, *piece.shape))).reshape(count, width)
    return mine, lax.ppermute(mine, "row", pairs)


def update_body(mine_ref, other_ref, f1_ref, f0_ref, xa_ref, xb_ref, p1_ref, p0_ref, out_ref, sum_ref, y_ref):
    width = p1_ref.shape[2]

    @pl.when(pl.program_id(0) == 0)
    def _():
        core = lax.axis_index("row") % 2
        rows = mine_ref.shape[0]
        sum_ref[pl.ds(pl.multiple_of(core * rows, 8), rows)] = mine_ref[...]
        sum_ref[pl.ds(pl.multiple_of((1 - core) * rows, 8), rows)] = other_ref[...]
        w1, w0, gram = (sum_ref[pl.ds(i * width, width)] for i in range(3))
        y1 = full(w1, f1_ref[...].reshape(width, width), ((1,), (1,)))
        w0 = w0 - full(y1, gram, ((1,), (0,)))
        y0 = full(w0, f0_ref[...].reshape(width, width), ((1,), (1,)))
        for i, y in enumerate((y1, y0)):
            high, low = parts_of(y)
            y_ref[i, 0] = high
            y_ref[i, 1] = low

    change = 0
    for i, ref in enumerate((p1_ref, p0_ref)):
        change += dot3((y_ref[i, 0], y_ref[i, 1]), parts_of(ref[0]), ((1,), (1,)))
    n, _, sub, rows = out_ref.shape
    for t, ref in enumerate((xa_ref, xb_ref)):
        half = ref.shape[0]
        out_ref[:, t] = (ref[...] - change[t * half : (t + 1) * half]).reshape(n, sub, rows)


def update(mine, other, fields, held, groups):
    width = held[0].shape[2]
    half, rows = fields[0].shape
    tiles = rows // GROUPS // TILE
    xspec = pl.BlockSpec((half, TILE), lambda i: (0, i))
    pspec = pl.BlockSpec((1, TILE, width), lambda i: (i // tiles, i % tiles, 0))
    extra = width // GROUPS
    fspec = pl.BlockSpec((GROUPS, extra, width), lambda i: (0, rows // GROUPS // extra, 0))
    whole = pl.BlockSpec(memory_space=pltpu.VMEM)
    return pl.pallas_call(
        update_body,
        out_shape=jax.ShapeDtypeStruct((groups, 2, half // groups, rows), F32),
        grid=(rows // TILE,),
        in_specs=[whole, whole, fspec, fspec, xspec, xspec, pspec, pspec],
        out_specs=pl.BlockSpec((groups, 2, half // groups, TILE), lambda i: (0, 0, 0, i)),
        scratch_shapes=[
            pltpu.VMEM((2 * mine.shape[0], width), F32),
            pltpu.VMEM((2, 2, width, width), jnp.bfloat16),
        ],
        compiler_params=pltpu.CompilerParams(vmem_limit_bytes=VMEM),
        name="update",
    )(mine, other, *held, *fields, *held)


def shards(eigvecs, reflectors, factors, owner):
    groups = lax.axis_size("row")
    own_count = eigvecs.shape[1]
    rows_here = eigvecs.shape[2] // groups
    width = factors.shape[2]
    half = own_count // 2

    size = sizes(reflectors, factors)[2]
    top = -(-2 * width // size) * size
    heads = []
    for block in BLOCKS:
        rows = lax.axis_index("row") * rows_here + lax.broadcasted_iota(jnp.int32, (top, width), 0)
        cols = lax.broadcasted_iota(jnp.int32, (top, width), 1) + block * width
        head = jnp.where(rows > cols, reflectors[0, :top], 0.0)
        heads.append(jnp.where(rows == cols, 1.0, head))
    held = None
    got = [None] * GROUPS
    crossed = [None] * GROUPS
    turns = [ring_pairs(step) for step in STEPS]
    swap = functools.partial(lax.all_to_all, axis_name="row", split_axis=0, concat_axis=0, tiled=True)
    fields = []
    splits = []
    wanted = {}
    for s in range(SLOTS + 1):
        for g in range(GROUPS):
            held, send, across, carried = slot_call(
                s, g, owner, reflectors, factors, heads, got[g], crossed[g], held,
                wanted.get((s, g), []), splits[1] if (s, g) == SECOND else None,
            )
            if send is not None:
                got[g] = [lax.ppermute(x, "col", turn) for x, turn in zip(send, turns)]
            if across is not None:
                crossed[g] = lax.ppermute(across, "col", SWAP)
            if (s, g) in ((0, GROUPS - 1), (1, GROUPS - 1)):
                splits.append(regroup(eigvecs, len(splits) * half, half, groups, send[0]))
                wanted[s + 1, 0] = [splits[-1]]
            if len(splits) == 1 and not fields:
                fields.append(swap(splits[0]).reshape(groups * half, rows_here))
                wanted[6, 0] = [fields[0]]
            if carried is not None:
                fields.append(swap(carried).reshape(groups * half, rows_here))

    mine, other = row_sum(*project(fields, held))
    return update(mine, other, fields, held, groups).reshape(1, own_count * groups, rows_here)


def solution(mesh):
    in_specs = (P("col", "row", None), P("col", "row", None), P("col", None, None), P())
    out_specs = P("col", None, "row")
    return jax.shard_map(shards, mesh=mesh, in_specs=in_specs, out_specs=out_specs, check_vma=False)
```

```python
import functools

import jax
import jax.numpy as jnp
from jax import lax
from jax.experimental import pallas as pl
from jax.experimental.pallas import tpu as pltpu
from jax.sharding import PartitionSpec as P

RING = 4
GROUPS = 2
QUARTER = 3
CHUNKS = RING * QUARTER
SLOTS = max(CHUNKS + 2, 3 * QUARTER + 5)
STEPS = (1, -1)
BLOCKS = (1, 0)
HEAD_SLOTS = 2
SECOND = (11, 1)
TILE = 2048
VMEM = 48 * 2**20
GRANT = 50 * 2**20
F32 = jnp.float32
ANY = pl.BlockSpec(memory_space=pl.ANY)
HBM = pl.BlockSpec(memory_space=pltpu.HBM)
SMEM = pl.BlockSpec(memory_space=pltpu.SMEM)


def ring_pairs(step):
    return [(h * RING + z, h * RING + (z + step) % RING) for h in range(2) for z in range(RING)]


SWAP = [(i, (i + RING) % (2 * RING)) for i in range(2 * RING)]


def sizes(own, factor):
    part, extra = own.shape[1] // GROUPS, factor.shape[1] // GROUPS
    assert (part + extra) % (CHUNKS * 8) == 0
    return part, extra, (part + extra) // CHUNKS


def crossing_id(batch, place):
    return jnp.where(place == 0, 3 * QUARTER + batch, 3 * batch + 3 - place)


def cross_slots(s):
    send = next((b for b in range(QUARTER) if s == 3 * b + 3), None)
    inject = next((b for b in range(QUARTER) if s == 3 * b + 5), None)
    return send, inject


def factor_slot(s):
    return s == CHUNKS - 1 or cross_slots(s)[0] == QUARTER - 1


def plan(s, owner, step):
    me = lax.axis_index("col")
    far = me // RING != owner // RING
    place = jnp.bitwise_and(step * (me - owner), RING - 1)
    source = me == owner
    _, inject = cross_slots(s)
    index = s - place
    keep = (index >= 0) & (index < CHUNKS) & ~far
    if s == 0:
        keep = source
    for b in range(QUARTER):
        j = s - 1 - (3 * b + 5)
        if 0 <= j < 3:
            index = jnp.where(far, crossing_id(b, jnp.bitwise_and(place - 1 - j, RING - 1)), index)
            keep = keep | far
    index = jnp.clip(index, 0, CHUNKS - 1)
    cross = crossing_id(inject, place) if inject is not None else 0
    return source, index, keep, far, cross


def slot_body(s, group, carried, shape, owner_ref, own_ref, *refs):
    refs = list(refs)
    over, inject = cross_slots(s)
    first = s == 0 and group == 0
    none = [None, None]
    factor_ref = refs.pop(0) if factor_slot(s) else None
    heads = [refs.pop(0), refs.pop(0)] if group == 0 and s < HEAD_SLOTS else none
    got = [refs.pop(0), refs.pop(0)] if s else none
    crossed = refs.pop(0) if inject is not None else None
    del refs[: carried + (0 if first else 2)]
    held = [refs.pop(0), refs.pop(0)]
    send = [refs.pop(0), refs.pop(0)] if s < SLOTS else none
    across = refs.pop(0) if over is not None else None
    del refs[: len(refs) - 2]
    stage, sems = refs
    part, extra, size = shape

    now, then = [], []
    for i in range(2):
        source, index, keep, far, cross = plan(s, owner_ref[BLOCKS[i]], STEPS[i])
        both = pl.ds(i * size, size)

        def bring(when, c, to):
            start, stop = c * size, min((c + 1) * size, part)
            if heads[i] is not None and stop <= heads[i].shape[0]:
                now.append((when, heads[i].at[pl.ds(start, size)], to))
                return
            src = own_ref.at[0, pl.ds(group * part + start, stop - start)]
            now.append((when, src, to.at[pl.ds(0, stop - start)]))
            if stop - start < size:
                src = factor_ref.at[0, pl.ds(group * extra, extra)]
                now.append((when, src, to.at[pl.ds(stop - start, extra)]))

        def slot(index):
            return held[i].at[group, pl.ds(pl.multiple_of(index * size, 8), size)]

        here, there = stage.at[i, 0], stage.at[i, 1]
        if s < CHUNKS:
            when = True if s == 0 else source
            bring(when, s, here)
            then.append((when, here, send[i]))
            then.append((source, here, slot(s)))
        passes = ~source if 0 < s < CHUNKS else True
        if inject is not None:
            now.append((far, crossed.at[both], send[i]))
            now.append((far, crossed.at[both], slot(cross)))
            passes = ~far if passes is True else passes & ~far
        if 0 < s < SLOTS:
            now.append((passes, got[i], send[i]))
        if s:
            now.append((keep & ~source, got[i], slot(index)))
        if over is not None:
            bring(source, 3 * QUARTER + over, there)
            then.append((source, there, across.at[both]))
            now.append((~source, got[i], across.at[both]))

    for copies in (now, then):
        for wait in (False, True):
            for n, (when, src, dst) in enumerate(copies):
                copy = pltpu.make_async_copy(src, dst, sems.at[n])
                act = copy.wait if wait else copy.start
                act() if when is True else pl.when(when)(act)


def slot_call(s, group, owner, own, factor, heads, got, crossed, held, wanted=(), carried=None):
    width = own.shape[2]
    part, extra, size = sizes(own, factor)
    over, inject = cross_slots(s)
    ins, specs = [owner, own], [SMEM, HBM]
    outs, out_specs = [jax.ShapeDtypeStruct((GROUPS, part + extra, width), own.dtype)] * 2, [HBM] * 2
    aliases = {}

    def add(arrays, spec):
        ins.extend(arrays)
        specs.extend([spec] * len(arrays))

    if factor_slot(s):
        add([factor], HBM)
    if group == 0 and s < HEAD_SLOTS:
        add(heads, ANY)
    if s:
        add(got, ANY)
    if inject is not None:
        add([crossed], ANY)
    add(wanted, ANY)
    if carried is not None:
        add([carried], HBM)
    if held is not None:
        aliases = {len(ins): 0, len(ins) + 1: 1}
        add(held, HBM)
    if s < SLOTS:
        outs += [jax.ShapeDtypeStruct((size, width), own.dtype)] * 2
    if over is not None:
        outs += [jax.ShapeDtypeStruct((2 * size, width), own.dtype)]
    out_specs += [ANY] * (len(outs) - 2)
    if carried is not None:
        aliases[len(ins) - 3] = len(outs)
        outs += [jax.ShapeDtypeStruct(carried.shape, carried.dtype)]
        out_specs += [HBM]
    out = pl.pallas_call(
        functools.partial(slot_body, s, group, len(wanted) + (carried is not None), (part, extra, size)),
        out_shape=outs,
        in_specs=specs,
        out_specs=out_specs,
        scratch_shapes=[pltpu.VMEM((2, 2, size, width), own.dtype), pltpu.SemaphoreType.DMA((20,))],
        input_output_aliases=aliases,
        compiler_params=pltpu.CompilerParams(vmem_limit_bytes=GRANT),
        cost_estimate=pl.CostEstimate(flops=0, bytes_accessed=4 * 2**20, transcendentals=0),
        name=f"slot{s}_{group}",
    )(*ins)
    out = list(out)
    held, out = out[:2], out[2:]
    send = [out.pop(0), out.pop(0)] if s < SLOTS else None
    across = out.pop(0) if over is not None else None
    return held, send, across, out.pop(0) if out else None


def begin_body(groups, owner_ref, own_ref, h1_ref, h0_ref, x_ref, *refs):
    held, send, split = refs[:2], refs[2:6], refs[6]
    stage, room, sems, own_sems = refs[7:]
    part, size, rows = own_ref.shape[1] // GROUPS, send[0].shape[0], split.shape[2]
    bring, give = [], []
    for i, head in enumerate((h1_ref, h0_ref)):
        source = lax.axis_index("col") == owner_ref[BLOCKS[i]]
        for g in range(GROUPS):
            src = head.at[pl.ds(0, size)] if g == 0 else own_ref.at[0, pl.ds(g * part, size)]
            here = stage.at[i, g]
            bring.append((True, src, here))
            give.append((True, here, send[2 * g + i]))
            give.append((source, here, held[i].at[g, pl.ds(0, size)]))

    def run(copies, base, wait):
        for n, (when, src, dst) in enumerate(copies):
            copy = pltpu.make_async_copy(src, dst, own_sems.at[base + n])
            act = copy.wait if wait else copy.start
            act() if when is True else pl.when(when)(act)

    def come(j):
        src = x_ref.at[0, pl.ds(0, split.shape[1]), pl.ds(j * rows, rows)]
        return pltpu.make_async_copy(src, room.at[j], sems.at[0, j])

    def leave(j):
        return pltpu.make_async_copy(room.at[j], split.at[j], sems.at[1, j])

    run(bring, 0, False)
    for j in range(groups):
        come(j).start()
    run(bring, 0, True)
    run(give, len(bring), False)
    for j in range(groups):
        come(j).wait()
        leave(j).start()
    run(give, len(bring), True)
    for j in range(groups):
        leave(j).wait()


def begin(owner, own, factor, heads, x, count, groups):
    width = own.shape[2]
    part, extra, size = sizes(own, factor)
    held = jax.ShapeDtypeStruct((GROUPS, part + extra, width), own.dtype)
    chunk = jax.ShapeDtypeStruct((size, width), own.dtype)
    split = jax.ShapeDtypeStruct((groups, count, x.shape[2] // groups), x.dtype)
    out = pl.pallas_call(
        functools.partial(begin_body, groups),
        out_shape=[held] * 2 + [chunk] * 4 + [split],
        in_specs=[SMEM, HBM, ANY, ANY, HBM],
        out_specs=[HBM] * 2 + [ANY] * 4 + [HBM],
        scratch_shapes=[
            pltpu.VMEM((2, GROUPS, size, width), own.dtype),
            pltpu.VMEM(split.shape, x.dtype),
            pltpu.SemaphoreType.DMA((2, groups)),
            pltpu.SemaphoreType.DMA((12,)),
        ],
        compiler_params=pltpu.CompilerParams(vmem_limit_bytes=GRANT),
        name="begin",
    )(owner, own, *heads, x)
    return out[:2], (out[2:4], out[4:6]), out[6]


def regroup_body(first, groups, x_ref, dep_ref, out_ref, room, sems):
    rows = out_ref.shape[2]

    def come(j):
        src = x_ref.at[0, pl.ds(first, out_ref.shape[1]), pl.ds(j * rows, rows)]
        return pltpu.make_async_copy(src, room.at[j], sems.at[0, j])

    def leave(j):
        return pltpu.make_async_copy(room.at[j], out_ref.at[j], sems.at[1, j])

    for j in range(groups):
        come(j).start()
    for j in range(groups):
        come(j).wait()
        leave(j).start()
    for j in range(groups):
        leave(j).wait()


def regroup(x, first, count, groups, dep):
    shape = (groups, count, x.shape[2] // groups)
    return pl.pallas_call(
        functools.partial(regroup_body, first, groups),
        out_shape=jax.ShapeDtypeStruct(shape, x.dtype),
        in_specs=[HBM, ANY],
        out_specs=HBM,
        scratch_shapes=[pltpu.VMEM(shape, x.dtype), pltpu.SemaphoreType.DMA((2, groups))],
        compiler_params=pltpu.CompilerParams(vmem_limit_bytes=GRANT),
        name="regroup",
    )(x, dep)


def parts_of(x):
    high = x.astype(jnp.bfloat16)
    low = (x - high.astype(F32)).astype(jnp.bfloat16)
    return high, low


def dot3(left, right, dims):
    (lh, ll), (rh, rl) = left, right
    go = functools.partial(lax.dot_general, dimension_numbers=(dims, ((), ())), preferred_element_type=F32)
    return go(lh, rh) + (go(lh, rl) + go(ll, rh))


def full(left, right, dims):
    return lax.dot_general(
        left, right, (dims, ((), ())), precision=lax.Precision.HIGHEST, preferred_element_type=F32
    )


def project_body(xa_ref, xb_ref, p1_ref, p0_ref, mine_ref, other_ref, sum_ref):
    half, width = xa_ref.shape[0], p1_ref.shape[2]
    p1, p0 = parts_of(p1_ref[0]), parts_of(p0_ref[0])

    @pl.when(pl.program_id(0) == 0)
    def _():
        sum_ref[...] = jnp.zeros_like(sum_ref)

    x = parts_of(jnp.concatenate([xa_ref[...], xb_ref[...]], 0))
    count = 2 * half
    sum_ref[pl.ds(0, count)] += dot3(x, p1, ((1,), (0,)))
    sum_ref[pl.ds(count, count)] += dot3(x, p0, ((1,), (0,)))
    sum_ref[pl.ds(2 * count, width)] += dot3(p1, p0, ((0,), (0,)))

    @pl.when(pl.program_id(0) == pl.num_programs(0) - 1)
    def _():
        core = lax.axis_index("row") % 2
        rows = mine_ref.shape[0]
        mine_ref[...] = sum_ref[pl.ds(pl.multiple_of(core * rows, 8), rows)]
        other_ref[...] = sum_ref[pl.ds(pl.multiple_of((1 - core) * rows, 8), rows)]


def project(fields, held):
    width = held[0].shape[2]
    half, rows = fields[0].shape
    tiles = rows // GROUPS // TILE
    xspec = pl.BlockSpec((half, TILE), lambda i: (0, i))
    pspec = pl.BlockSpec((1, TILE, width), lambda i: (i // tiles, i % tiles, 0))
    count = (4 * half + width) // 2
    return pl.pallas_call(
        project_body,
        out_shape=[jax.ShapeDtypeStruct((count, width), F32)] * 2,
        grid=(rows // TILE,),
        in_specs=[xspec, xspec, pspec, pspec],
        out_specs=[pl.BlockSpec((count, width), lambda i: (0, 0))] * 2,
        scratch_shapes=[pltpu.VMEM((2 * count, width), F32)],
        compiler_params=pltpu.CompilerParams(vmem_limit_bytes=VMEM),
        name="project",
    )(*fields, *held)


def row_sum(mine, other):
    devices = lax.axis_size("row")
    pairs = [(i, i ^ 1) for i in range(devices)]
    alike = [[i for i in range(devices) if i % 2 == core] for core in range(2)]
    swap = functools.partial(lax.all_to_all, axis_name="row", split_axis=0, concat_axis=0, tiled=True, axis_index_groups=alike)
    count, width = mine.shape
    chips = devices // 2
    mine = mine + lax.ppermute(other, "row", pairs)
    piece = jnp.sum(swap(mine.reshape(chips, count // chips, width)), 0)
    mine = swap(jnp.broadcast_to(piece, (chips, *piece.shape))).reshape(count, width)
    return mine, lax.ppermute(mine, "row", pairs)


def update_body(mine_ref, other_ref, f1_ref, f0_ref, xa_ref, xb_ref, p1_ref, p0_ref, out_ref, sum_ref, y_ref):
    width = p1_ref.shape[2]

    @pl.when(pl.program_id(0) == 0)
    def _():
        core = lax.axis_index("row") % 2
        rows = mine_ref.shape[0]
        sum_ref[pl.ds(pl.multiple_of(core * rows, 8), rows)] = mine_ref[...]
        sum_ref[pl.ds(pl.multiple_of((1 - core) * rows, 8), rows)] = other_ref[...]
        w1, w0, gram = (sum_ref[pl.ds(i * width, width)] for i in range(3))
        y1 = full(w1, f1_ref[...].reshape(width, width), ((1,), (1,)))
        w0 = w0 - full(y1, gram, ((1,), (0,)))
        y0 = full(w0, f0_ref[...].reshape(width, width), ((1,), (1,)))
        for i, y in enumerate((y1, y0)):
            high, low = parts_of(y)
            y_ref[i, 0] = high
            y_ref[i, 1] = low

    change = 0
    for i, ref in enumerate((p1_ref, p0_ref)):
        change += dot3((y_ref[i, 0], y_ref[i, 1]), parts_of(ref[0]), ((1,), (1,)))
    n, _, sub, rows = out_ref.shape
    for t, ref in enumerate((xa_ref, xb_ref)):
        half = ref.shape[0]
        out_ref[:, t] = (ref[...] - change[t * half : (t + 1) * half]).reshape(n, sub, rows)


def update(mine, other, fields, held, groups):
    width = held[0].shape[2]
    half, rows = fields[0].shape
    tiles = rows // GROUPS // TILE
    xspec = pl.BlockSpec((half, TILE), lambda i: (0, i))
    pspec = pl.BlockSpec((1, TILE, width), lambda i: (i // tiles, i % tiles, 0))
    extra = width // GROUPS
    fspec = pl.BlockSpec((GROUPS, extra, width), lambda i: (0, rows // GROUPS // extra, 0))
    whole = pl.BlockSpec(memory_space=pltpu.VMEM)
    return pl.pallas_call(
        update_body,
        out_shape=jax.ShapeDtypeStruct((groups, 2, half // groups, rows), F32),
        grid=(rows // TILE,),
        in_specs=[whole, whole, fspec, fspec, xspec, xspec, pspec, pspec],
        out_specs=pl.BlockSpec((groups, 2, half // groups, TILE), lambda i: (0, 0, 0, i)),
        scratch_shapes=[
            pltpu.VMEM((2 * mine.shape[0], width), F32),
            pltpu.VMEM((2, 2, width, width), jnp.bfloat16),
        ],
        compiler_params=pltpu.CompilerParams(vmem_limit_bytes=VMEM),
        name="update",
    )(mine, other, *held, *fields, *held)


def shards(eigvecs, reflectors, factors, owner):
    groups = lax.axis_size("row")
    own_count = eigvecs.shape[1]
    rows_here = eigvecs.shape[2] // groups
    width = factors.shape[2]
    half = own_count // 2

    size = sizes(reflectors, factors)[2]
    top = -(-2 * width // size) * size
    heads = []
    for block in BLOCKS:
        rows = lax.axis_index("row") * rows_here + lax.broadcasted_iota(jnp.int32, (top, width), 0)
        cols = lax.broadcasted_iota(jnp.int32, (top, width), 1) + block * width
        head = jnp.where(rows > cols, reflectors[0, :top], 0.0)
        heads.append(jnp.where(rows == cols, 1.0, head))
    turns = [ring_pairs(step) for step in STEPS]
    swap = functools.partial(lax.all_to_all, axis_name="row", split_axis=0, concat_axis=0, tiled=True)
    held, sends, split = begin(owner, reflectors, factors, heads, eigvecs, half, groups)
    got = [[lax.ppermute(x, "col", turn) for x, turn in zip(send, turns)] for send in sends]
    fields = [swap(split).reshape(groups * half, rows_here)]
    crossed = [None] * GROUPS
    wanted = {(6, 0): [fields[0]]}
    for s in range(1, SLOTS + 1):
        for g in range(GROUPS):
            held, send, across, carried = slot_call(
                s, g, owner, reflectors, factors, heads, got[g], crossed[g], held,
                wanted.get((s, g), []), split if (s, g) == SECOND else None,
            )
            if send is not None:
                got[g] = [lax.ppermute(x, "col", turn) for x, turn in zip(send, turns)]
            if across is not None:
                crossed[g] = lax.ppermute(across, "col", SWAP)
            if (s, g) == (1, GROUPS - 1):
                split = regroup(eigvecs, half, half, groups, send[0])
                wanted[2, 0] = [split]
            if carried is not None:
                fields.append(swap(carried).reshape(groups * half, rows_here))

    mine, other = row_sum(*project(fields, held))
    return update(mine, other, fields, held, groups).reshape(1, own_count * groups, rows_here)


def solution(mesh):
    in_specs = (P("col", "row", None), P("col", "row", None), P("col", None, None), P())
    out_specs = P("col", None, "row")
    return jax.shard_map(shards, mesh=mesh, in_specs=in_specs, out_specs=out_specs, check_vma=False)
```
